32 devices in a mesh: grp: 2 (over y), term: 4 (over z), sub: 2 (over x), pair: 2 (over core).
Axes of the slice: x: 2, y: 2, z: 4, core: 2. Of those that a mesh axis runs over, the one named last changes fastest.
Arguments:
- psi: bfloat16 [8, 256, 256], P(('grp', 'term'), 'pair'), parts along dimension 0, may hold values from -6 to 6
- left_blocks: bfloat16 [16, 8, 256, 256], P(('grp', 'term', 'sub'), None, 'pair'), parts along dimension 0, may hold values from -0.046875 to 0.046875
- right_blocks: bfloat16 [16, 8, 256, 256], P(('grp', 'term', 'sub')), parts along dimension 0, may hold values from -0.375 to 0.375
- left_index: int32 [16, 72], P(('grp', 'term', 'sub')), parts along dimension 0, may hold values from 0 to 7
- right_index: int32 [16, 72], P(('grp', 'term', 'sub')), parts along dimension 0, may hold values from 0 to 7
- block_source: int32 [16, 72], P(('grp', 'term', 'sub')), parts along dimension 0, may hold values from 0 to 3
- block_target: int32 [16, 72], P(('grp', 'term', 'sub')), parts along dimension 0, may hold values from 0 to 3
- block_count: int32 [16], P(('grp', 'term', 'sub')), parts along dimension 0, may hold values from 36 to 72, as said below
- sector_energy: float32 [8], P(('grp', 'term')), parts along dimension 0, may hold values from 0.3 to 3
Outputs:
- sigma_first: bfloat16 [8, 256, 256], P(('grp', 'term'), 'pair'), parts along dimension 0
- sigma_second: bfloat16 [8, 256, 256], P(('grp', 'term'), 'pair'), parts along dimension 0
The draws below stay inside these ranges and needn't reach their ends.
There are 2 independent parts, one for each index of `grp`. The reference program is written for one: setup_inputs(seed, part) draws one part's arguments, and reference() takes and returns one part's arrays. A program takes and returns all parts, laid end to end along the dimension named above; each array names one. Nothing has to cross between parts.
Inputs may be any that keep to these rules, and one draw needn't show every extreme that they name: `block_count`: some term sublist has all 72 slots live in every draw.
All inputs are finite; a program needn't handle non-finite values.
Results may differ from the reference program's by a relative error of at most 0.0074.
Values may be sent and summed in bfloat16 or wider, within the bound.
No kernel may reach another device: no remote copies, remote signals or barrier semaphores. Data moves between devices by JAX's collectives and lax.ppermute only.
A program may use at most 64 MiB of HBM per device.

```python
import math
import jax
import jax.numpy as jnp
from jax import lax

B = 256
NL = 8
NR = 8
NBLK_DEV = 72
SECTORS = 4
SUBLISTS = 8
N_SUB = 2


def draw_block_count(key, part):
    key = jax.random.fold_in(key, 7)
    first_key, second_key = jax.random.split(key)
    counts = jax.random.randint(first_key, (SUBLISTS,), max(1, NBLK_DEV // 2), NBLK_DEV + 1)
    chosen = jax.random.randint(second_key, (), 0, SUBLISTS)
    return jnp.where(jnp.arange(SUBLISTS) == chosen, NBLK_DEV, counts).astype(jnp.int32)


def set_ends(values, key, low, top_value):
    place = [jax.random.randint(jax.random.fold_in(key, axis), (), 0, length) for axis, length in enumerate(values.shape)]
    main_axis = values.shape.index(max(values.shape))
    neighbour = place[:main_axis] + [(place[main_axis] + 1) % values.shape[main_axis]] + place[main_axis + 1:]
    return values.at[tuple(place)].set(low).at[tuple(neighbour)].set(top_value)


def level_of(own_key, shape, cuts, low, high):
    gain = 1.0
    for dim, parts in cuts:
        draws = jax.random.uniform(jax.random.fold_in(jax.random.fold_in(own_key, 6), dim), (parts,), jnp.float32, low / len(cuts), high / len(cuts))
        gain = gain * jnp.repeat(jnp.exp(draws), shape[dim] // parts).reshape((-1,) + (1,) * (len(shape) - 1 - dim))
    return gain


def scatter_about(stream_key, extent, spread, reach, pieces=(), kind=jnp.bfloat16):
    array = jax.random.normal(stream_key, extent, jnp.float32) * spread
    if len(pieces) > 0:
        array = level_of(stream_key, extent, pieces, -0.22, 0.18) * array
    return jnp.clip(array, min=-reach, max=reach).astype(kind)


def setup_inputs(seed: int = 0, part: int = 0) -> dict:
    keys = jax.random.split(jax.random.key(seed), 10)
    part_splits = jax.random.split(jax.random.fold_in(keys[9], part), 10)
    psi = scatter_about(part_splits[0], (SECTORS, B, B), 1.0, 6.0, ((0, 4), (1, 2)))
    left_blocks = scatter_about(part_splits[1], (SUBLISTS, NL, B, B), (B * NBLK_DEV * N_SUB // 2) ** -0.5, 0.046875, ((0, 8), (2, 2)))
    right_blocks = scatter_about(part_splits[2], (SUBLISTS, NR, B, B), B ** -0.5, 0.375, ((0, 8),))
    left_index = set_ends(jax.random.randint(part_splits[3], (SUBLISTS, NBLK_DEV), 0, NL), jax.random.fold_in(part_splits[3], 1), 0, NL - 1).astype(jnp.int32)
    right_index = set_ends(jax.random.randint(part_splits[4], (SUBLISTS, NBLK_DEV), 0, NR), jax.random.fold_in(part_splits[4], 1), 0, NR - 1).astype(jnp.int32)
    block_source = set_ends(jax.random.randint(part_splits[5], (SUBLISTS, NBLK_DEV), 0, SECTORS), jax.random.fold_in(part_splits[5], 1), 0, SECTORS - 1).astype(jnp.int32)
    block_target = set_ends(jax.random.randint(part_splits[6], (SUBLISTS, NBLK_DEV), 0, SECTORS), jax.random.fold_in(part_splits[6], 1), 0, SECTORS - 1).astype(jnp.int32)
    block_count = draw_block_count(jax.random.fold_in(jax.random.fold_in(keys[9], part), 71), part)
    sector_energy = jnp.clip(jnp.exp(math.log(3.0) - 2.3025851 * jax.random.uniform(part_splits[8], (SECTORS,), jnp.float32) ** level_of(part_splits[8], (SECTORS,), ((0, 4),), -0.2, 0.2)), 0.3, 3.0)
    return dict(psi=psi, left_blocks=left_blocks, right_blocks=right_blocks, left_index=left_index, right_index=right_index, block_source=block_source, block_target=block_target, block_count=block_count, sector_energy=sector_energy)


def apply_hamiltonian(vector, left_blocks, right_blocks, left_index, right_index, block_source, block_target, block_count, sector_energy):

    def one_sublist(totals, item):
        lefts, rights, pick_left, pick_right, source, target, live_count = item
        left_part = jnp.take(lefts, pick_left, axis=0).astype(jnp.float32)
        right_part = jnp.take(rights, pick_right, axis=0).astype(jnp.float32)
        source_part = jnp.take(vector, source, axis=0).astype(jnp.float32)
        half = jnp.einsum('kij,kjl->kil', left_part, source_part).astype(jnp.bfloat16)
        half = lax.optimization_barrier(half).astype(jnp.float32)
        product = jnp.einsum('kil,kml->kim', half, right_part)
        alive = (jnp.arange(NBLK_DEV) < live_count).astype(jnp.float32)
        return (totals.at[target].add(product * alive[:, None, None]), None)
    start_totals = jnp.zeros((SECTORS, B, B), jnp.float32)
    items = (left_blocks, right_blocks, left_index, right_index, block_source, block_target, block_count)
    totals = lax.scan(one_sublist, start_totals, items)[0]
    return (totals + sector_energy[:, None, None] * vector.astype(jnp.float32)).astype(jnp.bfloat16)

def reference(psi, left_blocks, right_blocks, left_index, right_index, block_source, block_target, block_count, sector_energy):
    operands = (left_blocks, right_blocks, left_index, right_index, block_source, block_target, block_count, sector_energy)
    sigma_first = apply_hamiltonian(psi, *operands)
    vector = psi.astype(jnp.float32)
    sigma = sigma_first.astype(jnp.float32)
    theta = jnp.sum(vector * sigma) / jnp.sum(vector * vector)
    resid = sigma - theta * vector
    scale = lax.rsqrt(jnp.sum(resid * resid) / resid.size + 1e-06)
    correction = (resid * scale).astype(jnp.bfloat16)
    sigma_second = apply_hamiltonian(correction, *operands)
    return (sigma_first, sigma_second)
```

```python
import functools

import jax
import jax.numpy as jnp
from jax import lax
from jax.experimental import pallas as pl
from jax.experimental.pallas import tpu as pltpu
from jax.sharding import PartitionSpec as P

unroll_slots = 4
vmem_bytes = 48 * 1024 * 1024
whole_vmem = pl.BlockSpec(memory_space=pltpu.VMEM)
whole_smem = pl.BlockSpec(memory_space=pltpu.SMEM)


def plan_kernel(
    sectors, rights, lefts, me_ref, left_ref, right_ref, source_ref, target_ref, count_ref, plan_ref, next_ref
):
    me = me_ref[0]
    live = count_ref[0]
    groups = sectors * rights

    def group_of(slot):
        return (target_ref[0, slot] ^ me) * rights + right_ref[0, slot]

    def clear(group, carry):
        next_ref[group] = 0
        return carry

    def count(slot, carry):
        group = group_of(slot)
        next_ref[group] = next_ref[group] + 1
        return carry

    def start(group, total):
        size = next_ref[group]
        next_ref[group] = total
        return total + size

    def fill(slot, carry):
        group = group_of(slot)
        place = next_ref[group]
        next_ref[group] = place + 1
        half = (source_ref[0, slot] ^ me) * lefts + left_ref[0, slot]
        plan_ref[place] = half + group * 4096
        return carry

    def pad(place, carry):
        plan_ref[place] = groups * 4096
        return carry

    def mark(back, carry):
        place = live - 1 - back
        word = plan_ref[place]
        before = plan_ref[jnp.maximum(place - 1, 0)]
        same = (place > 0) & ((word // 4096) == (before // 4096))
        plan_ref[place] = word + jnp.where(same, 1 << 24, 0)
        return carry

    lax.fori_loop(0, groups, clear, 0)
    lax.fori_loop(0, live, count, 0)
    lax.fori_loop(0, groups, start, 0)
    lax.fori_loop(0, live, fill, 0)
    lax.fori_loop(live, plan_ref.shape[0], pad, 0)
    lax.fori_loop(0, live, mark, 0)


def make_plan(me, indices, block_count, sectors, lefts, rights):
    slots = indices[0].shape[1]
    padded = -(-slots // unroll_slots) * unroll_slots
    return pl.pallas_call(
        functools.partial(plan_kernel, sectors, rights, lefts),
        out_shape=jax.ShapeDtypeStruct((padded,), jnp.int32),
        in_specs=[whole_smem] * 6,
        out_specs=whole_smem,
        scratch_shapes=[pltpu.SMEM((sectors * rights,), jnp.int32)],
        cost_estimate=pl.CostEstimate(flops=4000000, bytes_accessed=4000000, transcendentals=0),
    )(me, *indices, block_count)


def multiply(sectors, live, plan_ref, left_ref, right_ref, vector, halves, sums, out_refs):
    lefts, half_rows, columns = left_ref.shape
    rights = right_ref.shape[0] // columns
    left_all = left_ref[...].reshape(lefts * half_rows, columns)
    sums[...] = jnp.zeros_like(sums)
    for j in range(sectors):
        half = jnp.dot(left_all, vector[j], preferred_element_type=jnp.float32)
        halves[j * lefts : (j + 1) * lefts] = half.astype(jnp.bfloat16).reshape(lefts, half_rows, columns)

    def some_slots(turn, total):
        for step in range(unroll_slots):
            word = plan_ref[turn * unroll_slots + step]
            half = word & 4095
            group = (word >> 12) & 4095
            keep = (word >> 24).astype(jnp.float32)
            row = pl.multiple_of((group // rights) * half_rows, half_rows)
            column = pl.multiple_of((group % rights) * columns, columns)
            total = total * keep + halves[half].astype(jnp.float32)
            sums[pl.ds(row, half_rows), pl.ds(column, columns)] = total.astype(jnp.bfloat16)
        return total

    turns = (live + unroll_slots - 1) // unroll_slots
    lax.fori_loop(0, turns, some_slots, jnp.zeros((half_rows, columns), jnp.float32))
    product = jnp.dot(sums[: sectors * half_rows], right_ref[...], preferred_element_type=jnp.float32)
    for j in range(sectors):
        out_refs[j][...] = product[j * half_rows : (j + 1) * half_rows].astype(out_refs[j].dtype)


def join(core, vector, j, mine, other):
    rows = mine.shape[0]
    vector[j, pl.ds(pl.multiple_of(core * rows, rows), rows)] = mine
    vector[j, pl.ds(pl.multiple_of((1 - core) * rows, rows), rows)] = other


def first_kernel(sectors, core_ref, count_ref, plan_ref, left_ref, right_ref, *refs):
    mine, other = refs[:sectors], refs[sectors : 2 * sectors]
    out_refs = refs[2 * sectors : 3 * sectors]
    vector, halves, sums = refs[3 * sectors :]
    for j in range(sectors):
        join(core_ref[0], vector, j, mine[j][...], other[j][...])
    multiply(sectors, count_ref[0], plan_ref, left_ref, right_ref, vector, halves, sums, out_refs)


def second_kernel(sectors, core_ref, count_ref, plan_ref, left_ref, right_ref, *refs):
    pieces = 2 * sectors
    psis, sigmas = refs[:pieces], refs[pieces : 2 * pieces]
    out_refs = refs[2 * pieces : 2 * pieces + sectors]
    own_ref = refs[2 * pieces + sectors]
    vector, halves, sums = refs[2 * pieces + sectors + 1 :]

    def wide(ref):
        return ref[...].astype(jnp.float32)

    norm = sum(wide(p) * wide(p) for p in psis)
    correlation = sum(wide(p) * wide(s) for p, s in zip(psis, sigmas))
    theta = jnp.sum(correlation) / jnp.sum(norm)
    square = jnp.zeros_like(norm)
    for p, s in zip(psis, sigmas):
        resid = wide(s) - theta * wide(p)
        square = square + resid * resid
    entries = pieces * norm.shape[0] * norm.shape[1]
    scale = lax.rsqrt(jnp.sum(square) / entries + 1e-06)
    for j in range(sectors):
        mine, other = (
            ((wide(sigmas[i]) - theta * wide(psis[i])) * scale).astype(jnp.bfloat16) for i in (j, sectors + j)
        )
        if j == 0:
            own_ref[...] = mine
        join(core_ref[0], vector, j, mine, other)
    multiply(sectors, count_ref[0], plan_ref, left_ref, right_ref, vector, halves, sums, out_refs)


def call_product(kernel, sectors, scalars, left, right, pieces, gives_own):
    lefts, half_rows, columns = left.shape
    rights = right.shape[0] // columns
    shape = (half_rows, columns)
    outs = [jax.ShapeDtypeStruct(shape, jnp.float32)]
    outs += [jax.ShapeDtypeStruct(shape, jnp.bfloat16)] * (sectors - 1 + gives_own)
    return pl.pallas_call(
        functools.partial(kernel, sectors),
        out_shape=outs,
        in_specs=[whole_smem] * len(scalars) + [whole_vmem] * (2 + len(pieces)),
        out_specs=[whole_vmem] * len(outs),
        scratch_shapes=[
            pltpu.VMEM((sectors, 2 * half_rows, columns), jnp.bfloat16),
            pltpu.VMEM((sectors * lefts, half_rows, columns), jnp.bfloat16),
            pltpu.VMEM(((sectors + 1) * half_rows, rights * columns), jnp.bfloat16),
        ],
        compiler_params=pltpu.CompilerParams(vmem_limit_bytes=vmem_bytes),
    )(*scalars, left, right, *pieces)


def swap(value, axis, bit):
    return lax.ppermute(value, axis, [(i, i ^ bit) for i in range(lax.axis_size(axis))])


def gather(own):
    sectors = lax.axis_size("term")
    mine = {0: own}
    for j in reversed(range(1, sectors)):
        mine[j] = swap(own, "term", j)
    other = {j: swap(mine[j], "pair", 1) for j in (0, *reversed(range(1, sectors)))}
    return [mine[j] for j in range(sectors)] + [other[j] for j in range(sectors)]


def owner_sum(parts):
    sent = {j: swap(parts[j], "term", j) for j in reversed(range(1, len(parts)))}
    total = parts[0]
    for j in range(1, len(parts)):
        total = total + sent[j].astype(jnp.float32)
    bit = 1
    while bit < lax.axis_size("sub"):
        rounded = total.astype(jnp.bfloat16)
        total = rounded.astype(jnp.float32) + swap(rounded, "sub", bit).astype(jnp.float32)
        bit *= 2
    return total


def on_device(
    psi,
    left_blocks,
    right_blocks,
    left_index,
    right_index,
    block_source,
    block_target,
    block_count,
    sector_energy,
):
    sectors = lax.axis_size("term")
    lefts, rights = left_blocks.shape[1], right_blocks.shape[1]
    me = lax.axis_index("term").astype(jnp.int32).reshape(1)
    core = lax.axis_index("pair").astype(jnp.int32).reshape(1)
    left = left_blocks[0]
    right = jnp.swapaxes(right_blocks[0], 1, 2).reshape(-1, right_blocks.shape[2])
    own = psi[0]
    psis = gather(own)
    plan = make_plan(
        me, (left_index, right_index, block_source, block_target), block_count, sectors, lefts, rights
    )
    scalars = (core, block_count, plan)
    parts = call_product(first_kernel, sectors, scalars, left, right, psis, False)
    energy = sector_energy[0]
    sigma_first = (owner_sum(parts) + energy * own.astype(jnp.float32)).astype(jnp.bfloat16)
    *parts, correction = call_product(
        second_kernel, sectors, scalars, left, right, psis + gather(sigma_first), True
    )
    sigma_second = (owner_sum(parts) + energy * correction.astype(jnp.float32)).astype(jnp.bfloat16)
    return (sigma_first[None], sigma_second[None])


def solution(mesh):
    placed = (
        P(("grp", "term"), "pair", None),
        P(("grp", "term", "sub"), None, "pair", None),
        P(("grp", "term", "sub"), None, None, None),
        P(("grp", "term", "sub"), None),
        P(("grp", "term", "sub"), None),
        P(("grp", "term", "sub"), None),
        P(("grp", "term", "sub"), None),
        P(("grp", "term", "sub")),
        P(("grp", "term")),
    )
    return jax.shard_map(
        on_device,
        mesh=mesh,
        in_specs=placed,
        out_specs=(P(("grp", "term"), "pair", None), P(("grp", "term"), "pair", None)),
        check_vma=False,
    )
```

```python
import functools

import jax
import jax.numpy as jnp
from jax import lax
from jax.experimental import pallas as pl
from jax.experimental.pallas import tpu as pltpu
from jax.sharding import PartitionSpec as P

unroll_slots = 4
wide_sectors = 4
step_lefts = 2
whole_vmem = pl.BlockSpec(memory_space=pltpu.VMEM)
whole_smem = pl.BlockSpec(memory_space=pltpu.SMEM)
stays_out = pl.BlockSpec(memory_space=pltpu.HBM)


def make_plan(me, left_index, right_index, source, target, live, sectors, lefts, rights):
    slots = left_index.shape[0]
    padded = -(-slots // unroll_slots) * unroll_slots
    number = jnp.arange(slots, dtype=jnp.int32)
    alive = number < live
    group = jnp.where(alive, right_index * sectors + (target ^ me), rights * sectors)
    half = jnp.where(alive, (source ^ me) * lefts + left_index, 0)
    same = group[None, :] == group[:, None]
    before = number[None, :] < number[:, None]
    place = jnp.sum(((group[None, :] < group[:, None]) | (same & before)).astype(jnp.int32), axis=1)
    goes_on = jnp.max((same & before).astype(jnp.int32), axis=1)
    word = half + (group << 12) + (goes_on << 24)
    put = place[None, :] == jnp.arange(padded, dtype=jnp.int32)[:, None]
    empty = jnp.arange(padded, dtype=jnp.int32) >= slots
    return jnp.sum(jnp.where(put, word[None, :], 0), axis=1) + jnp.where(empty, (rights * sectors) << 12, 0)


def multiply(sectors, live, plan_ref, copies, left_ref, right_ref, vector, halves, sums, out_refs):
    lefts, half_rows, columns = left_ref.shape
    rights = right_ref.shape[0]
    left_all = left_ref.reshape(lefts * half_rows, columns)
    sums[...] = jnp.zeros_like(sums)
    copies[1].wait()
    for first in range(0, sectors, wide_sectors):
        chosen = range(first, min(first + wide_sectors, sectors))
        wide = jnp.concatenate([vector[j] for j in chosen], axis=1)
        for left in range(0, lefts, step_lefts):
            rows = left_all[left * half_rows : (left + step_lefts) * half_rows, :]
            half = jnp.dot(rows, wide, preferred_element_type=jnp.float32).astype(jnp.bfloat16)
            for place, j in enumerate(chosen):
                part = half[:, place * columns : (place + 1) * columns]
                halves[j * lefts + left : j * lefts + left + step_lefts] = part.reshape(-1, half_rows, columns)

    def some_slots(turn, total):
        for step in range(unroll_slots):
            word = plan_ref[turn * unroll_slots + step]
            keep = (word >> 24).astype(jnp.float32)
            total = total * keep + halves[word & 4095].astype(jnp.float32)
            sums[(word >> 12) & 4095] = total.astype(jnp.bfloat16)
        return total

    turns = (live + unroll_slots - 1) // unroll_slots
    lax.fori_loop(0, turns, some_slots, jnp.zeros((half_rows, columns), jnp.float32))
    copies[2].wait()
    product = 0
    for r in range(rights):
        rows = sums[r * sectors : (r + 1) * sectors].reshape(sectors * half_rows, columns)
        product = product + lax.dot_general(
            rows, right_ref[r], (((1,), (1,)), ((), ())), preferred_element_type=jnp.float32
        )
    for j in range(sectors):
        out_refs[j][...] = product[j * half_rows : (j + 1) * half_rows].astype(out_refs[j].dtype)


def join(core, vector, j, mine, other):
    rows = mine.shape[0]
    vector[j, pl.ds(pl.multiple_of(core * rows, rows), rows)] = mine
    vector[j, pl.ds(pl.multiple_of((1 - core) * rows, rows), rows)] = other


def fetch(sources, places, arrived):
    copies = [pltpu.make_async_copy(*pair, arrived.at[i]) for i, pair in enumerate(zip(sources, places))]
    for copy in copies:
        copy.start()
    return copies


def first_kernel(sectors, core_ref, count_ref, plan_ref, left_hbm, right_hbm, own_hbm, *refs):
    mine, other = refs[: sectors - 1], refs[sectors - 1 : 2 * sectors - 1]
    out_refs = refs[2 * sectors - 1 : 3 * sectors - 1]
    left, right, own, arrived, vector, halves, sums = refs[3 * sectors - 1 :]
    copies = fetch((own_hbm, left_hbm, right_hbm), (own, left, right), arrived)
    for j in range(1, sectors):
        join(core_ref[0], vector, j, mine[j - 1][...], other[j][...])
    copies[0].wait()
    join(core_ref[0], vector, 0, own[...], other[0][...])
    multiply(sectors, count_ref[0], plan_ref, copies, left, right, vector, halves, sums, out_refs)


def second_kernel(sectors, core_ref, count_ref, plan_ref, left_hbm, right_hbm, own_hbm, *refs):
    pieces = 2 * sectors
    psis, sigmas = refs[: pieces - 1], refs[pieces - 1 : 2 * pieces - 1]
    out_refs = refs[2 * pieces - 1 : 2 * pieces + sectors - 1]
    own_ref = refs[2 * pieces + sectors - 1]
    left, right, own, arrived, vector, halves, sums = refs[2 * pieces + sectors :]
    copies = fetch((own_hbm, left_hbm, right_hbm), (own, left, right), arrived)
    copies[0].wait()
    psis = (own, *psis)

    def wide(ref):
        return ref[...].astype(jnp.float32)

    norm = sum(wide(p) * wide(p) for p in psis)
    correlation = sum(wide(p) * wide(s) for p, s in zip(psis, sigmas))
    theta = jnp.sum(correlation) / jnp.sum(norm)
    square = jnp.zeros_like(norm)
    for p, s in zip(psis, sigmas):
        resid = wide(s) - theta * wide(p)
        square = square + resid * resid
    entries = pieces * norm.shape[0] * norm.shape[1]
    scale = lax.rsqrt(jnp.sum(square) / entries + 1e-06)
    for j in range(sectors):
        mine, other = (
            ((wide(sigmas[i]) - theta * wide(psis[i])) * scale).astype(jnp.bfloat16) for i in (j, sectors + j)
        )
        if j == 0:
            own_ref[...] = mine
        join(core_ref[0], vector, j, mine, other)
    multiply(sectors, count_ref[0], plan_ref, copies, left, right, vector, halves, sums, out_refs)


def call_product(kernel, sectors, scalars, left, right, pieces, gives_own):
    lefts, half_rows, columns = left.shape
    rights = right.shape[0]
    shape = (half_rows, columns)
    block_bytes = half_rows * columns * 2
    outs = [jax.ShapeDtypeStruct(shape, jnp.float32)]
    outs += [jax.ShapeDtypeStruct(shape, jnp.bfloat16)] * (sectors - 1 + gives_own)
    return pl.pallas_call(
        functools.partial(kernel, sectors),
        out_shape=outs,
        in_specs=[whole_smem] * len(scalars) + [stays_out] * 3 + [whole_vmem] * (len(pieces) - 1),
        out_specs=[whole_vmem] * len(outs),
        scratch_shapes=[
            pltpu.VMEM(left.shape, jnp.bfloat16),
            pltpu.VMEM(right.shape, jnp.bfloat16),
            pltpu.VMEM(shape, jnp.bfloat16),
            pltpu.SemaphoreType.DMA((3,)),
            pltpu.VMEM((sectors, 2 * half_rows, columns), jnp.bfloat16),
            pltpu.VMEM((sectors * lefts, half_rows, columns), jnp.bfloat16),
            pltpu.VMEM((sectors * rights + 1, half_rows, columns), jnp.bfloat16),
        ],
        compiler_params=pltpu.CompilerParams(
            vmem_limit_bytes=block_bytes * (sectors * (lefts + rights + 24) + 64)
        ),
    )(*scalars, *(pltpu.with_memory_space_constraint(x, pltpu.HBM) for x in (left, right, pieces[0])), *pieces[1:])


def swap(value, axis, bit):
    return lax.ppermute(value, axis, [(i, i ^ bit) for i in range(lax.axis_size(axis))])


def gather(own):
    sectors = lax.axis_size("term")
    mine = {0: own}
    for j in reversed(range(1, sectors)):
        mine[j] = swap(own, "term", j)
    other = {j: swap(mine[j], "pair", 1) for j in (0, *reversed(range(1, sectors)))}
    return [mine[j] for j in range(sectors)] + [other[j] for j in range(sectors)]


def owner_sum(parts):
    sent = {j: swap(parts[j], "term", j) for j in reversed(range(1, len(parts)))}
    total = parts[0]
    for j in range(1, len(parts)):
        total = total + sent[j].astype(jnp.float32)
    bit = 1
    while bit < lax.axis_size("sub"):
        rounded = total.astype(jnp.bfloat16)
        total = rounded.astype(jnp.float32) + swap(rounded, "sub", bit).astype(jnp.float32)
        bit *= 2
    return total


def on_device(
    psi,
    left_blocks,
    right_blocks,
    left_index,
    right_index,
    block_source,
    block_target,
    block_count,
    sector_energy,
):
    sectors = lax.axis_size("term")
    lefts, rights = left_blocks.shape[1], right_blocks.shape[1]
    me = lax.axis_index("term").astype(jnp.int32)
    core = lax.axis_index("pair").astype(jnp.int32).reshape(1)
    left = left_blocks[0]
    right = right_blocks[0]
    own = psi[0]
    psis = gather(own)
    indices = (left_index[0], right_index[0], block_source[0], block_target[0])
    plan = make_plan(me, *indices, block_count[0], sectors, lefts, rights)
    scalars = (core, block_count, plan)
    parts = call_product(first_kernel, sectors, scalars, left, right, psis, False)
    energy = sector_energy[0]
    sigma_first = (owner_sum(parts) + energy * own.astype(jnp.float32)).astype(jnp.bfloat16)
    *parts, correction = call_product(
        second_kernel, sectors, scalars, left, right, psis + gather(sigma_first), True
    )
    sigma_second = (owner_sum(parts) + energy * correction.astype(jnp.float32)).astype(jnp.bfloat16)
    return (sigma_first[None], sigma_second[None])


def solution(mesh):
    placed = (
        P(("grp", "term"), "pair", None),
        P(("grp", "term", "sub"), None, "pair", None),
        P(("grp", "term", "sub"), None, None, None),
        P(("grp", "term", "sub"), None),
        P(("grp", "term", "sub"), None),
        P(("grp", "term", "sub"), None),
        P(("grp", "term", "sub"), None),
        P(("grp", "term", "sub")),
        P(("grp", "term")),
    )
    return jax.shard_map(
        on_device,
        mesh=mesh,
        in_specs=placed,
        out_specs=(P(("grp", "term"), "pair", None), P(("grp", "term"), "pair", None)),
        check_vma=False,
    )
```

```python
import functools

import jax
import jax.numpy as jnp
from jax import lax
from jax.experimental import pallas as pl
from jax.experimental.pallas import tpu as pltpu
from jax.sharding import PartitionSpec as P

unroll_slots = 4
wide_sectors = 4
step_lefts = 2
whole_vmem = pl.BlockSpec(memory_space=pltpu.VMEM)
whole_smem = pl.BlockSpec(memory_space=pltpu.SMEM)
stays_out = pl.BlockSpec(memory_space=pltpu.HBM)


def make_plan(me, left_index, right_index, source, target, live, sectors, lefts, rights):
    slots = left_index.shape[0]
    padded = -(-slots // unroll_slots) * unroll_slots
    number = jnp.arange(slots, dtype=jnp.int32)
    alive = number < live
    group = jnp.where(alive, right_index * sectors + (target ^ me), rights * sectors)
    half = jnp.where(alive, (source ^ me) * lefts + left_index, 0)
    same = group[None, :] == group[:, None]
    before = number[None, :] < number[:, None]
    place = jnp.sum(((group[None, :] < group[:, None]) | (same & before)).astype(jnp.int32), axis=1)
    goes_on = jnp.max((same & before).astype(jnp.int32), axis=1)
    word = half + (group << 12) + (goes_on << 24)
    put = place[None, :] == jnp.arange(padded, dtype=jnp.int32)[:, None]
    empty = jnp.arange(padded, dtype=jnp.int32) >= slots
    return jnp.sum(jnp.where(put, word[None, :], 0), axis=1) + jnp.where(empty, (rights * sectors) << 12, 0)


def half_products(sectors, left_ref, vector, halves):
    lefts, half_rows, columns = left_ref.shape
    left_all = left_ref.reshape(lefts * half_rows, columns)
    for first in range(0, sectors, wide_sectors):
        chosen = range(first, min(first + wide_sectors, sectors))
        wide = jnp.concatenate([vector[j] for j in chosen], axis=1)
        for left in range(0, lefts, step_lefts):
            rows = left_all[left * half_rows : (left + step_lefts) * half_rows, :]
            half = jnp.dot(rows, wide, preferred_element_type=jnp.float32).astype(jnp.bfloat16)
            for place, j in enumerate(chosen):
                part = half[:, place * columns : (place + 1) * columns]
                halves[j * lefts + left : j * lefts + left + step_lefts] = part.reshape(-1, half_rows, columns)


def sum_halves(live, plan_ref, halves, sums):
    def some_slots(turn, total):
        for step in range(unroll_slots):
            word = plan_ref[turn * unroll_slots + step]
            keep = (word >> 24).astype(jnp.float32)
            total = total * keep + halves[word & 4095].astype(jnp.float32)
            sums[(word >> 12) & 4095] = total.astype(jnp.bfloat16)
        return total

    turns = (live + unroll_slots - 1) // unroll_slots
    lax.fori_loop(0, turns, some_slots, jnp.zeros(halves.shape[1:], jnp.float32))


def all_targets(sectors, right_ref, sums, out_refs):
    half_rows, columns = sums.shape[1:]
    product = 0
    for r in range(right_ref.shape[0]):
        rows = sums[r * sectors : (r + 1) * sectors].reshape(sectors * half_rows, columns)
        product = product + lax.dot_general(
            rows, right_ref[r], (((1,), (1,)), ((), ())), preferred_element_type=jnp.float32
        )
    for j in range(sectors):
        out_refs[j][...] = product[j * half_rows : (j + 1) * half_rows].astype(out_refs[j].dtype)


def join(core, vector, j, mine, other):
    rows = mine.shape[0]
    vector[j, pl.ds(pl.multiple_of(core * rows, rows), rows)] = mine
    vector[j, pl.ds(pl.multiple_of((1 - core) * rows, rows), rows)] = other


def wide_of(ref):
    return ref[...].astype(jnp.float32)


def fetch_kernel(*refs):
    arrived = refs[-1]
    count = len(refs) // 2
    copies = [pltpu.make_async_copy(refs[i], refs[count + i], arrived.at[i]) for i in range(count)]
    for copy in copies:
        copy.start()
    for copy in copies:
        copy.wait()


def fetch(*arrays):
    return pl.pallas_call(
        fetch_kernel,
        out_shape=[pltpu.VMEM(x.shape, x.dtype) for x in arrays],
        in_specs=[stays_out] * len(arrays),
        out_specs=[whole_vmem] * len(arrays),
        scratch_shapes=[pltpu.SemaphoreType.DMA((len(arrays),))],
    )(*(pltpu.with_memory_space_constraint(x, pltpu.HBM) for x in arrays))


def first_kernel(sectors, core_ref, count_ref, plan_ref, left, right, *refs):
    psis, out_refs = refs[: 2 * sectors], refs[2 * sectors : -3]
    vector, halves, sums = refs[-3:]
    sums[...] = jnp.zeros_like(sums)
    for j in range(sectors):
        join(core_ref[0], vector, j, psis[j][...], psis[sectors + j][...])
    half_products(sectors, left, vector, halves)
    sum_halves(count_ref[0], plan_ref, halves, sums)
    all_targets(sectors, right, sums, out_refs)


def second_kernel(sectors, core_ref, count_ref, plan_ref, left, right, *refs):
    pieces = 2 * sectors
    psis, sigmas = refs[:pieces], refs[pieces : 2 * pieces]
    own_ref, *out_refs = refs[2 * pieces : -3]
    vector, halves, sums = refs[-3:]
    sums[...] = jnp.zeros_like(sums)
    norm = sum(wide_of(p) * wide_of(p) for p in psis)
    correlation = sum(wide_of(p) * wide_of(s) for p, s in zip(psis, sigmas))
    theta = jnp.sum(correlation) / jnp.sum(norm)
    square = jnp.zeros_like(norm)
    for p, s in zip(psis, sigmas):
        resid = wide_of(s) - theta * wide_of(p)
        square = square + resid * resid
    entries = pieces * norm.shape[0] * norm.shape[1]
    scale = lax.rsqrt(jnp.sum(square) / entries + 1e-06)
    for j in range(sectors):
        mine, other = (
            ((wide_of(sigmas[i]) - theta * wide_of(psis[i])) * scale).astype(jnp.bfloat16) for i in (j, sectors + j)
        )
        if j == 0:
            own_ref[...] = mine
        join(core_ref[0], vector, j, mine, other)
    half_products(sectors, left, vector, halves)
    sum_halves(count_ref[0], plan_ref, halves, sums)
    all_targets(sectors, right, sums, out_refs)


def call_product(kernel, sectors, lefts, rights, scalars, inside, kept):
    half_rows, columns = inside[-1].shape
    shape = (half_rows, columns)
    block_bytes = half_rows * columns * 2
    outs = [*kept, pltpu.VMEM(shape, jnp.float32)] + [pltpu.VMEM(shape, jnp.bfloat16)] * (sectors - 1)
    return pl.pallas_call(
        functools.partial(kernel, sectors),
        out_shape=outs,
        in_specs=[whole_smem] * len(scalars) + [whole_vmem] * len(inside),
        out_specs=[whole_vmem] * len(outs),
        scratch_shapes=[
            pltpu.VMEM((sectors, 2 * half_rows, columns), jnp.bfloat16),
            pltpu.VMEM((sectors * lefts, half_rows, columns), jnp.bfloat16),
            pltpu.VMEM((sectors * rights + 1, half_rows, columns), jnp.bfloat16),
        ],
        compiler_params=pltpu.CompilerParams(
            vmem_limit_bytes=block_bytes * (sectors * (lefts + rights + 24) + 64)
        ),
    )(
        *scalars,
        *(pltpu.with_memory_space_constraint(x, pltpu.VMEM) for x in inside),
    )


def swap(value, axis, bit):
    return lax.ppermute(value, axis, [(i, i ^ bit) for i in range(lax.axis_size(axis))])


def gather(own, kept):
    sectors = lax.axis_size("term")
    mine = {0: kept}
    for j in reversed(range(1, sectors)):
        mine[j] = swap(own, "term", j)
    other = {j: swap(mine[j], "pair", 1) for j in (0, *reversed(range(1, sectors)))}
    return [mine[j] for j in range(sectors)] + [other[j] for j in range(sectors)]


def owner_sum(parts):
    sent = {j: swap(parts[j], "term", j) for j in reversed(range(1, len(parts)))}
    total = parts[0]
    for j in range(1, len(parts)):
        total = total + sent[j].astype(jnp.float32)
    bit = 1
    while bit < lax.axis_size("sub"):
        rounded = total.astype(jnp.bfloat16)
        total = rounded.astype(jnp.float32) + swap(rounded, "sub", bit).astype(jnp.float32)
        bit *= 2
    return total


def on_device(
    psi,
    left_blocks,
    right_blocks,
    left_index,
    right_index,
    block_source,
    block_target,
    block_count,
    sector_energy,
):
    sectors = lax.axis_size("term")
    lefts, rights = left_blocks.shape[1], right_blocks.shape[1]
    me = lax.axis_index("term").astype(jnp.int32)
    core = lax.axis_index("pair").astype(jnp.int32).reshape(1)
    own = psi[0]
    left, right, own_kept = fetch(left_blocks[0], right_blocks[0], own)
    psis = gather(own, own_kept)
    indices = (left_index[0], right_index[0], block_source[0], block_target[0])
    plan = make_plan(me, *indices, block_count[0], sectors, lefts, rights)
    energy = sector_energy[0]
    call = functools.partial(
        call_product, sectors=sectors, lefts=lefts, rights=rights, scalars=(core, block_count, plan)
    )
    parts = call(first_kernel, inside=[left, right, *psis], kept=[])
    sigma_first = (owner_sum(parts) + energy * own.astype(jnp.float32)).astype(jnp.bfloat16)
    correction, *parts = call(
        second_kernel,
        inside=[left, right, *psis, *gather(sigma_first, sigma_first)],
        kept=[pltpu.VMEM(own.shape, own.dtype)],
    )
    sigma_second = (owner_sum(parts) + energy * correction.astype(jnp.float32)).astype(jnp.bfloat16)
    return (sigma_first[None], sigma_second[None])


def solution(mesh):
    placed = (
        P(("grp", "term"), "pair", None),
        P(("grp", "term", "sub"), None, "pair", None),
        P(("grp", "term", "sub"), None, None, None),
        P(("grp", "term", "sub"), None),
        P(("grp", "term", "sub"), None),
        P(("grp", "term", "sub"), None),
        P(("grp", "term", "sub"), None),
        P(("grp", "term", "sub")),
        P(("grp", "term")),
    )
    return jax.shard_map(
        on_device,
        mesh=mesh,
        in_specs=placed,
        out_specs=(P(("grp", "term"), "pair", None), P(("grp", "term"), "pair", None)),
        check_vma=False,
    )
```

```python
import functools

import jax
import jax.numpy as jnp
from jax import lax
from jax.experimental import pallas as pl
from jax.experimental.pallas import tpu as pltpu
from jax.sharding import PartitionSpec as P

four_order = [0, 2, 1, 3]
direct_distances = (3,)
unroll_slots = 4
wide_sectors = 4
step_lefts = 2
whole_vmem = pl.BlockSpec(memory_space=pltpu.VMEM)
stays_out = pl.BlockSpec(memory_space=pltpu.HBM)


def target_order(sectors):
    return four_order if sectors == 4 else list(range(sectors))


def plan_length(slots):
    return -(-(slots + unroll_slots) // 128) * 128


def make_plan(me, left_index, right_index, source, target, live, sectors, lefts, rights):
    slots = left_index.shape[0]
    length = plan_length(slots)
    number = jnp.arange(slots, dtype=jnp.int32)
    alive = number < live
    distance = target ^ me
    sent_at = sum(jnp.where(distance == far, place, 0) for place, far in enumerate(target_order(sectors)))
    group = jnp.where(alive, right_index * sectors + sent_at, rights * sectors)
    half = jnp.where(alive, (source ^ me) * lefts + left_index, 0)
    same = group[None, :] == group[:, None]
    before = number[None, :] < number[:, None]
    place = jnp.sum(((group[None, :] < group[:, None]) | (same & before)).astype(jnp.int32), axis=1)
    goes_on = jnp.max((same & before).astype(jnp.int32), axis=1)
    word = half + (group << 12) + (goes_on << 24)
    at = jnp.arange(length, dtype=jnp.int32)
    sorted_words = jnp.sum(jnp.where(place[None, :] == at[:, None], word[None, :], 0), axis=1)
    rest = jnp.where(at == length - 1, live, (rights * sectors) << 12)
    return jnp.where(at < slots, sorted_words, rest)[None]


def half_products(sectors, left_ref, vector, halves):
    lefts, half_rows, columns = left_ref.shape
    left_all = left_ref.reshape(lefts * half_rows, columns)
    for first in range(0, sectors, wide_sectors):
        chosen = range(first, min(first + wide_sectors, sectors))
        wide = jnp.concatenate([vector[j] for j in chosen], axis=1)
        for left in range(0, lefts, step_lefts):
            rows = left_all[left * half_rows : (left + step_lefts) * half_rows, :]
            half = jnp.dot(rows, wide, preferred_element_type=jnp.float32).astype(jnp.bfloat16)
            for place, j in enumerate(chosen):
                part = half[:, place * columns : (place + 1) * columns]
                part = part.reshape(-1, half_rows, columns).astype(jnp.float32)
                halves[j * lefts + left : j * lefts + left + step_lefts] = part


def sum_halves(plan_ref, halves, sums):
    live = plan_ref[0, plan_ref.shape[1] - 1]

    def some_slots(turn, total):
        for step in range(unroll_slots):
            word = plan_ref[0, turn * unroll_slots + step]
            keep = (word >> 24).astype(jnp.float32)
            total = total * keep + halves[word & 4095]
            sums[(word >> 12) & 4095] = total.astype(jnp.bfloat16)
        return total

    turns = (live + unroll_slots - 1) // unroll_slots
    lax.fori_loop(0, turns, some_slots, jnp.zeros(halves.shape[1:], jnp.float32))


def all_targets(sectors, right_ref, sums, out_refs):
    half_rows, columns = sums.shape[1:]
    product = 0
    for r in range(right_ref.shape[0]):
        rows = sums[r * sectors : (r + 1) * sectors].reshape(sectors * half_rows, columns)
        product = product + lax.dot_general(
            rows, right_ref[r], (((1,), (1,)), ((), ())), preferred_element_type=jnp.float32
        )
    for j in range(sectors):
        out_refs[j][...] = product[j * half_rows : (j + 1) * half_rows].astype(out_refs[j].dtype)


def join(core, vector, j, mine, other):
    rows = mine.shape[0]
    vector[j, pl.ds(pl.multiple_of(core * rows, rows), rows)] = mine
    vector[j, pl.ds(pl.multiple_of((1 - core) * rows, rows), rows)] = other


def wide_of(ref):
    return ref[...].astype(jnp.float32)


def fetch_kernel(*refs):
    arrived = refs[-1]
    count = len(refs) // 2
    copies = [pltpu.make_async_copy(refs[i], refs[count + i], arrived.at[i]) for i in range(count)]
    for copy in copies:
        copy.start()
    for copy in copies:
        copy.wait()


def fetch(*arrays):
    return pl.pallas_call(
        fetch_kernel,
        out_shape=[pltpu.VMEM(x.shape, x.dtype) for x in arrays],
        in_specs=[stays_out] * len(arrays),
        out_specs=[whole_vmem] * len(arrays),
        scratch_shapes=[pltpu.SemaphoreType.DMA((len(arrays),))],
    )(*(pltpu.with_memory_space_constraint(x, pltpu.HBM) for x in arrays))


def first_kernel(sectors, plan_in, left, right, *refs):
    psis, out_refs = refs[: 2 * sectors], refs[2 * sectors : -5]
    plan_ref, arrived, vector, halves, sums = refs[-5:]
    core = lax.axis_index("pair")
    plan_copy = pltpu.make_async_copy(plan_in, plan_ref, arrived)
    plan_copy.start()
    sums[...] = jnp.zeros_like(sums)
    for j in range(sectors):
        join(core, vector, j, psis[j][...], psis[sectors + j][...])
    half_products(sectors, left, vector, halves)
    plan_copy.wait()
    sum_halves(plan_ref, halves, sums)
    all_targets(sectors, right, sums, out_refs)


def second_kernel(sectors, plan_in, left, right, *refs):
    pieces = 2 * sectors
    psis, sigmas = refs[:pieces], refs[pieces : 2 * pieces]
    own_ref, *out_refs = refs[2 * pieces : -5]
    plan_ref, arrived, vector, halves, sums = refs[-5:]
    core = lax.axis_index("pair")
    plan_copy = pltpu.make_async_copy(plan_in, plan_ref, arrived)
    plan_copy.start()
    sums[...] = jnp.zeros_like(sums)
    norm = sum(wide_of(p) * wide_of(p) for p in psis)
    correlation = sum(wide_of(p) * wide_of(s) for p, s in zip(psis, sigmas))
    theta = jnp.sum(correlation) / jnp.sum(norm)
    square = jnp.zeros_like(norm)
    for p, s in zip(psis, sigmas):
        resid = wide_of(s) - theta * wide_of(p)
        square = square + resid * resid
    entries = pieces * norm.shape[0] * norm.shape[1]
    scale = lax.rsqrt(jnp.sum(square) / entries + 1e-06)
    for j in range(sectors):
        mine, other = (
            ((wide_of(sigmas[i]) - theta * wide_of(psis[i])) * scale).astype(jnp.bfloat16) for i in (j, sectors + j)
        )
        if j == 0:
            own_ref[...] = mine
        join(core, vector, j, mine, other)
    half_products(sectors, left, vector, halves)
    plan_copy.wait()
    sum_halves(plan_ref, halves, sums)
    all_targets(sectors, right, sums, out_refs)


def call_product(kernel, sectors, lefts, rights, inside, kept):
    half_rows, columns = inside[-1].shape
    shape = (half_rows, columns)
    block_bytes = half_rows * columns * 2
    outs = [*kept, pltpu.VMEM(shape, jnp.float32)] + [pltpu.VMEM(shape, jnp.bfloat16)] * (sectors - 1)
    return pl.pallas_call(
        functools.partial(kernel, sectors),
        out_shape=outs,
        in_specs=[whole_vmem] * len(inside),
        out_specs=[whole_vmem] * len(outs),
        scratch_shapes=[
            pltpu.SMEM(inside[0].shape, jnp.int32),
            pltpu.SemaphoreType.DMA,
            pltpu.VMEM((sectors, 2 * half_rows, columns), jnp.bfloat16),
            pltpu.VMEM((sectors * lefts, half_rows, columns), jnp.float32),
            pltpu.VMEM((sectors * rights + 1, half_rows, columns), jnp.bfloat16),
        ],
        compiler_params=pltpu.CompilerParams(
            vmem_limit_bytes=block_bytes * (sectors * (2 * lefts + rights + 24) + 64)
        ),
    )(*(pltpu.with_memory_space_constraint(x, pltpu.VMEM) for x in inside))


def swap(value, axis, bit):
    return lax.ppermute(value, axis, [(i, i ^ bit) for i in range(lax.axis_size(axis))])


def gather(own, kept):
    sectors = lax.axis_size("term")
    mine = {0: kept}
    for j in reversed(range(1, sectors)):
        mine[j] = swap(own, "term", j)
    other = {j: swap(mine[j], "pair", 1) for j in (0, *reversed(range(1, sectors)))}
    return [mine[j] for j in range(sectors)] + [other[j] for j in range(sectors)]


def send(value, far, across):
    sectors, subs = lax.axis_size("term"), lax.axis_size("sub")
    route = [(t * subs + s, (t ^ far) * subs + (s ^ across)) for t in range(sectors) for s in range(subs)]
    return lax.ppermute(value, ("term", "sub"), route)


def owner_sum(parts):
    subs = lax.axis_size("sub")
    order = target_order(len(parts))
    direct = [far for far in order if far in direct_distances and subs == 2 and len(parts) == 4]
    total = parts[0]
    for place, far in enumerate(order):
        if place > 0 and far not in direct:
            total = total + send(parts[place], far, 0).astype(jnp.float32)
    beside = [send(parts[order.index(far)], far, across).astype(jnp.float32) for far in direct for across in range(subs)]
    bit = 1
    while bit < subs:
        rounded = total.astype(jnp.bfloat16)
        total = rounded.astype(jnp.float32) + send(rounded, 0, bit).astype(jnp.float32)
        bit *= 2
    for one, two in zip(beside[::2], beside[1::2]):
        total = total + (one + two)
    return total


def on_device(
    psi,
    left_blocks,
    right_blocks,
    left_index,
    right_index,
    block_source,
    block_target,
    block_count,
    sector_energy,
):
    sectors = lax.axis_size("term")
    lefts, rights = left_blocks.shape[1], right_blocks.shape[1]
    me = lax.axis_index("term").astype(jnp.int32)
    own = psi[0]
    left, right, own_kept = fetch(left_blocks[0], right_blocks[0], own)
    psis = gather(own, own_kept)
    indices = (left_index[0], right_index[0], block_source[0], block_target[0])
    plan = make_plan(me, *indices, block_count[0], sectors, lefts, rights)
    energy = sector_energy[0]
    call = functools.partial(call_product, sectors=sectors, lefts=lefts, rights=rights)
    parts = call(first_kernel, inside=[plan, left, right, *psis], kept=[])
    sigma_first = (owner_sum(parts) + energy * own.astype(jnp.float32)).astype(jnp.bfloat16)
    correction, *parts = call(
        second_kernel,
        inside=[plan, left, right, *psis, *gather(sigma_first, sigma_first)],
        kept=[pltpu.VMEM(own.shape, own.dtype)],
    )
    sigma_second = (owner_sum(parts) + energy * correction.astype(jnp.float32)).astype(jnp.bfloat16)
    return (sigma_first[None], sigma_second[None])


def solution(mesh):
    placed = (
        P(("grp", "term"), "pair", None),
        P(("grp", "term", "sub"), None, "pair", None),
        P(("grp", "term", "sub"), None, None, None),
        P(("grp", "term", "sub"), None),
        P(("grp", "term", "sub"), None),
        P(("grp", "term", "sub"), None),
        P(("grp", "term", "sub"), None),
        P(("grp", "term", "sub")),
        P(("grp", "term")),
    )
    return jax.shard_map(
        on_device,
        mesh=mesh,
        in_specs=placed,
        out_specs=(P(("grp", "term"), "pair", None), P(("grp", "term"), "pair", None)),
        check_vma=False,
    )
```

```python
import functools

import jax
import jax.numpy as jnp
from jax import lax
from jax.experimental import pallas as pl
from jax.experimental.pallas import tpu as pltpu
from jax.sharding import PartitionSpec as P

gather_four = [0, 1, 3, 2]
target_four = [0, 2, 1, 3]
direct_distances = (3,)
unroll_slots = 4
wide_sectors = 4
step_lefts = 2
whole_vmem = pl.BlockSpec(memory_space=pltpu.VMEM)
stays_out = pl.BlockSpec(memory_space=pltpu.HBM)


def gather_order(sectors):
    return gather_four if sectors == 4 else list(range(sectors))


def target_order(sectors):
    return target_four if sectors == 4 else list(range(sectors))


def place_in(order, distance):
    return sum(jnp.where(distance == far, place, 0) for place, far in enumerate(order))


def plan_length(slots):
    return -(-(slots + unroll_slots) // 128) * 128


def make_plan(me, left_index, right_index, source, target, live, sectors, lefts, rights):
    slots = left_index.shape[0]
    length = plan_length(slots)
    number = jnp.arange(slots, dtype=jnp.int32)
    alive = number < live
    sent_at = place_in(target_order(sectors), target ^ me)
    group = jnp.where(alive, right_index * sectors + sent_at, rights * sectors)
    half = jnp.where(alive, place_in(gather_order(sectors), source ^ me) * lefts + left_index, 0)
    same = group[None, :] == group[:, None]
    before = number[None, :] < number[:, None]
    place = jnp.sum(((group[None, :] < group[:, None]) | (same & before)).astype(jnp.int32), axis=1)
    goes_on = jnp.max((same & before).astype(jnp.int32), axis=1)
    word = half + (group << 12) + (goes_on << 24)
    at = jnp.arange(length, dtype=jnp.int32)
    sorted_words = jnp.sum(jnp.where(place[None, :] == at[:, None], word[None, :], 0), axis=1)
    rest = jnp.where(at == length - 1, live, (rights * sectors) << 12)
    return jnp.where(at < slots, sorted_words, rest)[None]


def half_products(sectors, left_ref, vector, halves):
    lefts, half_rows, columns = left_ref.shape
    left_all = left_ref.reshape(lefts * half_rows, columns)
    for first in range(0, sectors, wide_sectors):
        chosen = range(first, min(first + wide_sectors, sectors))
        wide = jnp.concatenate([vector[j] for j in chosen], axis=1)
        for left in range(0, lefts, step_lefts):
            rows = left_all[left * half_rows : (left + step_lefts) * half_rows, :]
            half = jnp.dot(rows, wide, preferred_element_type=jnp.float32).astype(jnp.bfloat16)
            for place, j in enumerate(chosen):
                part = half[:, place * columns : (place + 1) * columns]
                part = part.reshape(-1, half_rows, columns).astype(jnp.float32)
                halves[j * lefts + left : j * lefts + left + step_lefts] = part


def sum_halves(plan_ref, halves, sums):
    live = plan_ref[0, plan_ref.shape[1] - 1]

    def some_slots(turn, total):
        for step in range(unroll_slots):
            word = plan_ref[0, turn * unroll_slots + step]
            keep = (word >> 24).astype(jnp.float32)
            total = total * keep + halves[word & 4095]
            sums[(word >> 12) & 4095] = total.astype(jnp.bfloat16)
        return total

    turns = (live + unroll_slots - 1) // unroll_slots
    lax.fori_loop(0, turns, some_slots, jnp.zeros(halves.shape[1:], jnp.float32))


def all_targets(sectors, right_ref, sums, out_refs):
    half_rows, columns = sums.shape[1:]
    product = 0
    for r in range(right_ref.shape[0]):
        rows = sums[r * sectors : (r + 1) * sectors].reshape(sectors * half_rows, columns)
        product = product + lax.dot_general(
            rows, right_ref[r], (((1,), (1,)), ((), ())), preferred_element_type=jnp.float32
        )
    for j in range(sectors):
        out_refs[j][...] = product[j * half_rows : (j + 1) * half_rows].astype(out_refs[j].dtype)


def join(core, vector, j, mine, other):
    rows = mine.shape[0]
    vector[j, pl.ds(pl.multiple_of(core * rows, rows), rows)] = mine
    vector[j, pl.ds(pl.multiple_of((1 - core) * rows, rows), rows)] = other


def wide_of(ref):
    return ref[...].astype(jnp.float32)


def fetch_kernel(*refs):
    arrived = refs[-1]
    count = len(refs) // 2
    copies = [pltpu.make_async_copy(refs[i], refs[count + i], arrived.at[i]) for i in range(count)]
    for copy in copies:
        copy.start()
    for copy in copies:
        copy.wait()


def fetch(*arrays):
    return pl.pallas_call(
        fetch_kernel,
        out_shape=[pltpu.VMEM(x.shape, x.dtype) for x in arrays],
        in_specs=[stays_out] * len(arrays),
        out_specs=[whole_vmem] * len(arrays),
        scratch_shapes=[pltpu.SemaphoreType.DMA((len(arrays),))],
    )(*(pltpu.with_memory_space_constraint(x, pltpu.HBM) for x in arrays))


def first_kernel(sectors, plan_in, left, right, *refs):
    psis, out_refs = refs[: 2 * sectors], refs[2 * sectors : -5]
    plan_ref, arrived, vector, halves, sums = refs[-5:]
    core = lax.axis_index("pair")
    plan_copy = pltpu.make_async_copy(plan_in, plan_ref, arrived)
    plan_copy.start()
    sums[...] = jnp.zeros_like(sums)
    for j in range(sectors):
        join(core, vector, j, psis[j][...], psis[sectors + j][...])
    half_products(sectors, left, vector, halves)
    plan_copy.wait()
    sum_halves(plan_ref, halves, sums)
    all_targets(sectors, right, sums, out_refs)


def second_kernel(sectors, plan_in, left, right, *refs):
    pieces = 2 * sectors
    psis, sigmas = refs[:pieces], refs[pieces : 2 * pieces]
    own_ref, *out_refs = refs[2 * pieces : -5]
    plan_ref, arrived, vector, halves, sums = refs[-5:]
    core = lax.axis_index("pair")
    plan_copy = pltpu.make_async_copy(plan_in, plan_ref, arrived)
    plan_copy.start()
    sums[...] = jnp.zeros_like(sums)
    norm = sum(wide_of(p) * wide_of(p) for p in psis)
    correlation = sum(wide_of(p) * wide_of(s) for p, s in zip(psis, sigmas))
    theta = jnp.sum(correlation) / jnp.sum(norm)
    square = jnp.zeros_like(norm)
    for p, s in zip(psis, sigmas):
        resid = wide_of(s) - theta * wide_of(p)
        square = square + resid * resid
    entries = pieces * norm.shape[0] * norm.shape[1]
    scale = lax.rsqrt(jnp.sum(square) / entries + 1e-06)
    for j in range(sectors):
        mine, other = (
            ((wide_of(sigmas[i]) - theta * wide_of(psis[i])) * scale).astype(jnp.bfloat16) for i in (j, sectors + j)
        )
        if j == 0:
            own_ref[...] = mine
        join(core, vector, j, mine, other)
    half_products(sectors, left, vector, halves)
    plan_copy.wait()
    sum_halves(plan_ref, halves, sums)
    all_targets(sectors, right, sums, out_refs)


def call_product(kernel, sectors, lefts, rights, inside, kept):
    half_rows, columns = inside[-1].shape
    shape = (half_rows, columns)
    block_bytes = half_rows * columns * 2
    outs = [*kept, pltpu.VMEM(shape, jnp.float32)] + [pltpu.VMEM(shape, jnp.bfloat16)] * (sectors - 1)
    return pl.pallas_call(
        functools.partial(kernel, sectors),
        out_shape=outs,
        in_specs=[whole_vmem] * len(inside),
        out_specs=[whole_vmem] * len(outs),
        scratch_shapes=[
            pltpu.SMEM(inside[0].shape, jnp.int32),
            pltpu.SemaphoreType.DMA,
            pltpu.VMEM((sectors, 2 * half_rows, columns), jnp.bfloat16),
            pltpu.VMEM((sectors * lefts, half_rows, columns), jnp.float32),
            pltpu.VMEM((sectors * rights + 1, half_rows, columns), jnp.bfloat16),
        ],
        compiler_params=pltpu.CompilerParams(
            vmem_limit_bytes=block_bytes * (sectors * (2 * lefts + rights + 24) + 64)
        ),
    )(*(pltpu.with_memory_space_constraint(x, pltpu.VMEM) for x in inside))


def swap(value, axis, bit):
    return lax.ppermute(value, axis, [(i, i ^ bit) for i in range(lax.axis_size(axis))])


def gather(own, kept):
    sectors = lax.axis_size("term")
    order = gather_order(sectors)
    mine = {0: kept}
    for j in reversed(range(1, sectors)):
        mine[j] = swap(own, "term", order[j])
    other = {j: swap(mine[j], "pair", 1) for j in (0, *reversed(range(1, sectors)))}
    return [mine[j] for j in range(sectors)] + [other[j] for j in range(sectors)]


def send(value, far, across):
    sectors, subs = lax.axis_size("term"), lax.axis_size("sub")
    route = [(t * subs + s, (t ^ far) * subs + (s ^ across)) for t in range(sectors) for s in range(subs)]
    return lax.ppermute(value, ("term", "sub"), route)


def owner_sum(parts):
    subs = lax.axis_size("sub")
    order = target_order(len(parts))
    direct = [far for far in order if far in direct_distances and subs == 2 and len(parts) == 4]
    total = parts[0]
    for place, far in enumerate(order):
        if place > 0 and far not in direct:
            total = total + send(parts[place], far, 0).astype(jnp.float32)
    beside = [send(parts[order.index(far)], far, across).astype(jnp.float32) for far in direct for across in range(subs)]
    bit = 1
    while bit < subs:
        rounded = total.astype(jnp.bfloat16)
        total = rounded.astype(jnp.float32) + send(rounded, 0, bit).astype(jnp.float32)
        bit *= 2
    for one, two in zip(beside[::2], beside[1::2]):
        total = total + (one + two)
    return total


def on_device(
    psi,
    left_blocks,
    right_blocks,
    left_index,
    right_index,
    block_source,
    block_target,
    block_count,
    sector_energy,
):
    sectors = lax.axis_size("term")
    lefts, rights = left_blocks.shape[1], right_blocks.shape[1]
    me = lax.axis_index("term").astype(jnp.int32)
    own = psi[0]
    left, right, own_kept = fetch(left_blocks[0], right_blocks[0], own)
    psis = gather(own, own_kept)
    indices = (left_index[0], right_index[0], block_source[0], block_target[0])
    plan = make_plan(me, *indices, block_count[0], sectors, lefts, rights)
    energy = sector_energy[0]
    call = functools.partial(call_product, sectors=sectors, lefts=lefts, rights=rights)
    parts = call(first_kernel, inside=[plan, left, right, *psis], kept=[])
    sigma_first = (owner_sum(parts) + energy * own.astype(jnp.float32)).astype(jnp.bfloat16)
    correction, *parts = call(
        second_kernel,
        inside=[plan, left, right, *psis, *gather(sigma_first, sigma_first)],
        kept=[pltpu.VMEM(own.shape, own.dtype)],
    )
    sigma_second = (owner_sum(parts) + energy * correction.astype(jnp.float32)).astype(jnp.bfloat16)
    return (sigma_first[None], sigma_second[None])


def solution(mesh):
    placed = (
        P(("grp", "term"), "pair", None),
        P(("grp", "term", "sub"), None, "pair", None),
        P(("grp", "term", "sub"), None, None, None),
        P(("grp", "term", "sub"), None),
        P(("grp", "term", "sub"), None),
        P(("grp", "term", "sub"), None),
        P(("grp", "term", "sub"), None),
        P(("grp", "term", "sub")),
        P(("grp", "term")),
    )
    return jax.shard_map(
        on_device,
        mesh=mesh,
        in_specs=placed,
        out_specs=(P(("grp", "term"), "pair", None), P(("grp", "term"), "pair", None)),
        check_vma=False,
    )
```

```python
import functools

import jax
import jax.numpy as jnp
from jax import lax
from jax.experimental import pallas as pl
from jax.experimental.pallas import tpu as pltpu
from jax.sharding import PartitionSpec as P

gather_four = [0, 1, 3, 2]
target_four = [0, 2, 1, 3]
direct_distances = (3,)
unroll_slots = 3
wide_sectors = 4
step_lefts = 2
whole_vmem = pl.BlockSpec(memory_space=pltpu.VMEM)
stays_out = pl.BlockSpec(memory_space=pltpu.HBM)


def gather_order(sectors):
    return gather_four if sectors == 4 else list(range(sectors))


def target_order(sectors):
    return target_four if sectors == 4 else list(range(sectors))


def place_in(order, distance):
    return sum(jnp.where(distance == far, place, 0) for place, far in enumerate(order))


def plan_length(slots):
    return -(-(slots + unroll_slots) // 128) * 128


def make_plan(me, left_index, right_index, source, target, live, sectors, lefts, rights):
    slots = left_index.shape[0]
    length = plan_length(slots)
    number = jnp.arange(slots, dtype=jnp.int32)
    alive = number < live
    sent_at = place_in(target_order(sectors), target ^ me)
    group = jnp.where(alive, right_index * sectors + sent_at, rights * sectors)
    half = jnp.where(alive, place_in(gather_order(sectors), source ^ me) * lefts + left_index, 0)
    same = group[None, :] == group[:, None]
    before = number[None, :] < number[:, None]
    place = jnp.sum(((group[None, :] < group[:, None]) | (same & before)).astype(jnp.int32), axis=1)
    goes_on = jnp.max((same & before).astype(jnp.int32), axis=1)
    word = half + (group << 12) + (goes_on << 24)
    at = jnp.arange(length, dtype=jnp.int32)
    sorted_words = jnp.sum(jnp.where(place[None, :] == at[:, None], word[None, :], 0), axis=1)
    rest = jnp.where(at == length - 1, live, (rights * sectors) << 12)
    return jnp.where(at < slots, sorted_words, rest)[None]


def half_products(sectors, left_ref, vector, halves):
    lefts, half_rows, columns = left_ref.shape
    left_all = left_ref.reshape(lefts * half_rows, columns)
    for first in range(0, sectors, wide_sectors):
        chosen = range(first, min(first + wide_sectors, sectors))
        wide = jnp.concatenate([vector[j] for j in chosen], axis=1)
        for left in range(0, lefts, step_lefts):
            rows = left_all[left * half_rows : (left + step_lefts) * half_rows, :]
            half = jnp.dot(rows, wide, preferred_element_type=jnp.float32).astype(jnp.bfloat16)
            for place, j in enumerate(chosen):
                part = half[:, place * columns : (place + 1) * columns]
                part = part.reshape(-1, half_rows, columns).astype(jnp.float32)
                halves[j * lefts + left : j * lefts + left + step_lefts] = part


def sum_halves(plan_ref, halves, sums):
    live = plan_ref[0, plan_ref.shape[1] - 1]

    def some_slots(turn, total):
        for step in range(unroll_slots):
            word = plan_ref[0, turn * unroll_slots + step]
            keep = (word >> 24).astype(jnp.float32)
            total = total * keep + halves[word & 4095]
            sums[(word >> 12) & 4095] = total.astype(jnp.bfloat16)
        return total

    turns = (live + unroll_slots - 1) // unroll_slots
    lax.fori_loop(0, turns, some_slots, jnp.zeros(halves.shape[1:], jnp.float32))


def all_targets(sectors, right_ref, sums, out_refs):
    half_rows, columns = sums.shape[1:]
    product = 0
    for r in range(right_ref.shape[0]):
        rows = sums[r * sectors : (r + 1) * sectors].reshape(sectors * half_rows, columns)
        product = product + lax.dot_general(
            rows, right_ref[r], (((1,), (1,)), ((), ())), preferred_element_type=jnp.float32
        )
    for j in range(sectors):
        out_refs[j][...] = product[j * half_rows : (j + 1) * half_rows].astype(out_refs[j].dtype)


def join(core, vector, j, mine, other):
    rows = mine.shape[0]
    vector[j, pl.ds(pl.multiple_of(core * rows, rows), rows)] = mine
    vector[j, pl.ds(pl.multiple_of((1 - core) * rows, rows), rows)] = other


def wide_of(ref):
    return ref[...].astype(jnp.float32)


def fetch_kernel(*refs):
    arrived = refs[-1]
    count = len(refs) // 2
    copies = [pltpu.make_async_copy(refs[i], refs[count + i], arrived.at[i]) for i in range(count)]
    for copy in copies:
        copy.start()
    for copy in copies:
        copy.wait()


def fetch(*arrays):
    return pl.pallas_call(
        fetch_kernel,
        out_shape=[pltpu.VMEM(x.shape, x.dtype) for x in arrays],
        in_specs=[stays_out] * len(arrays),
        out_specs=[whole_vmem] * len(arrays),
        scratch_shapes=[pltpu.SemaphoreType.DMA((len(arrays),))],
    )(*(pltpu.with_memory_space_constraint(x, pltpu.HBM) for x in arrays))


def first_kernel(sectors, plan_in, left, right, *refs):
    psis = refs[: 2 * sectors]
    norm_ref, *out_refs = refs[2 * sectors : -5]
    plan_ref, arrived, vector, halves, sums = refs[-5:]
    core = lax.axis_index("pair")
    plan_copy = pltpu.make_async_copy(plan_in, plan_ref, arrived)
    plan_copy.start()
    sums[...] = jnp.zeros_like(sums)
    for j in range(sectors):
        join(core, vector, j, psis[j][...], psis[sectors + j][...])
    norm = sum(wide_of(p) * wide_of(p) for p in psis)
    norm_ref[...] = jnp.sum(norm.reshape(-1, 8, norm.shape[1]), axis=0)
    half_products(sectors, left, vector, halves)
    plan_copy.wait()
    sum_halves(plan_ref, halves, sums)
    all_targets(sectors, right, sums, out_refs)


def second_kernel(sectors, plan_in, left, right, norm_ref, *refs):
    pieces = 2 * sectors
    psis, sigmas = refs[:pieces], refs[pieces : 2 * pieces]
    own_ref, *out_refs = refs[2 * pieces : -5]
    plan_ref, arrived, vector, halves, sums = refs[-5:]
    resids = halves
    core = lax.axis_index("pair")
    plan_copy = pltpu.make_async_copy(plan_in, plan_ref, arrived)
    plan_copy.start()
    sums[...] = jnp.zeros_like(sums)
    correlation = sum(wide_of(p) * wide_of(s) for p, s in zip(psis, sigmas))
    theta = jnp.sum(correlation) / jnp.sum(norm_ref[...])
    square = 0
    for i, (p, s) in enumerate(zip(psis, sigmas)):
        resid = wide_of(s) - theta * wide_of(p)
        resids[i] = resid
        square = square + resid * resid
    scale = lax.rsqrt(jnp.sum(square) / (pieces * square.shape[0] * square.shape[1]) + 1e-06)
    for j in range(sectors):
        mine, other = ((resids[i] * scale).astype(jnp.bfloat16) for i in (j, sectors + j))
        if j == 0:
            own_ref[...] = mine
        join(core, vector, j, mine, other)
    half_products(sectors, left, vector, halves)
    plan_copy.wait()
    sum_halves(plan_ref, halves, sums)
    all_targets(sectors, right, sums, out_refs)


def call_product(kernel, sectors, lefts, rights, inside, kept):
    half_rows, columns = inside[-1].shape
    shape = (half_rows, columns)
    block_bytes = half_rows * columns * 2
    outs = [*kept, pltpu.VMEM(shape, jnp.float32)] + [pltpu.VMEM(shape, jnp.bfloat16)] * (sectors - 1)
    return pl.pallas_call(
        functools.partial(kernel, sectors),
        out_shape=outs,
        in_specs=[whole_vmem] * len(inside),
        out_specs=[whole_vmem] * len(outs),
        scratch_shapes=[
            pltpu.SMEM(inside[0].shape, jnp.int32),
            pltpu.SemaphoreType.DMA,
            pltpu.VMEM((sectors, 2 * half_rows, columns), jnp.bfloat16),
            pltpu.VMEM((sectors * lefts, half_rows, columns), jnp.float32),
            pltpu.VMEM((sectors * rights + 1, half_rows, columns), jnp.bfloat16),
        ],
        compiler_params=pltpu.CompilerParams(
            vmem_limit_bytes=block_bytes * (sectors * (2 * lefts + rights + 24) + 64)
        ),
    )(*(pltpu.with_memory_space_constraint(x, pltpu.VMEM) for x in inside))


def swap(value, axis, bit):
    return lax.ppermute(value, axis, [(i, i ^ bit) for i in range(lax.axis_size(axis))])


def gather(own, kept):
    sectors = lax.axis_size("term")
    order = gather_order(sectors)
    mine = {0: kept}
    for j in reversed(range(1, sectors)):
        mine[j] = swap(own, "term", order[j])
    other = {j: swap(mine[j], "pair", 1) for j in (0, *reversed(range(1, sectors)))}
    return [mine[j] for j in range(sectors)] + [other[j] for j in range(sectors)]


def send(value, far, across):
    sectors, subs = lax.axis_size("term"), lax.axis_size("sub")
    route = [(t * subs + s, (t ^ far) * subs + (s ^ across)) for t in range(sectors) for s in range(subs)]
    return lax.ppermute(value, ("term", "sub"), route)


def owner_sum(parts):
    subs = lax.axis_size("sub")
    order = target_order(len(parts))
    direct = [far for far in order if far in direct_distances and subs == 2 and len(parts) == 4]
    total = parts[0]
    for place, far in enumerate(order):
        if place > 0 and far not in direct:
            total = total + send(parts[place], far, 0).astype(jnp.float32)
    beside = [send(parts[order.index(far)], far, across).astype(jnp.float32) for far in direct for across in range(subs)]
    bit = 1
    while bit < subs:
        rounded = total.astype(jnp.bfloat16)
        total = rounded.astype(jnp.float32) + send(rounded, 0, bit).astype(jnp.float32)
        bit *= 2
    for one, two in zip(beside[::2], beside[1::2]):
        total = total + (one + two)
    return total


def on_device(
    psi,
    left_blocks,
    right_blocks,
    left_index,
    right_index,
    block_source,
    block_target,
    block_count,
    sector_energy,
):
    sectors = lax.axis_size("term")
    lefts, rights = left_blocks.shape[1], right_blocks.shape[1]
    me = lax.axis_index("term").astype(jnp.int32)
    own = psi[0]
    left, right, own_kept = fetch(left_blocks[0], right_blocks[0], own)
    psis = gather(own, own_kept)
    indices = (left_index[0], right_index[0], block_source[0], block_target[0])
    plan = make_plan(me, *indices, block_count[0], sectors, lefts, rights)
    energy = sector_energy[0]
    call = functools.partial(call_product, sectors=sectors, lefts=lefts, rights=rights)
    norm, *parts = call(
        first_kernel, inside=[plan, left, right, *psis], kept=[pltpu.VMEM((8, own.shape[1]), jnp.float32)]
    )
    sigma_first = (owner_sum(parts) + energy * own.astype(jnp.float32)).astype(jnp.bfloat16)
    correction, *parts = call(
        second_kernel,
        inside=[plan, left, right, norm, *psis, *gather(sigma_first, sigma_first)],
        kept=[pltpu.VMEM(own.shape, own.dtype)],
    )
    sigma_second = (owner_sum(parts) + energy * correction.astype(jnp.float32)).astype(jnp.bfloat16)
    return (sigma_first[None], sigma_second[None])


def solution(mesh):
    placed = (
        P(("grp", "term"), "pair", None),
        P(("grp", "term", "sub"), None, "pair", None),
        P(("grp", "term", "sub"), None, None, None),
        P(("grp", "term", "sub"), None),
        P(("grp", "term", "sub"), None),
        P(("grp", "term", "sub"), None),
        P(("grp", "term", "sub"), None),
        P(("grp", "term", "sub")),
        P(("grp", "term")),
    )
    return jax.shard_map(
        on_device,
        mesh=mesh,
        in_specs=placed,
        out_specs=(P(("grp", "term"), "pair", None), P(("grp", "term"), "pair", None)),
        check_vma=False,
    )
```

```python
import functools

import jax
import jax.numpy as jnp
from jax import lax
from jax.experimental import pallas as pl
from jax.experimental.pallas import tpu as pltpu
from jax.sharding import PartitionSpec as P

gather_four = [0, 1, 3, 2]
target_four = [0, 2, 1, 3]
direct_distances = (3,)
first_four = [0, 1, 3, 2]
unroll_slots = 4
group_bit, last_bit = 8, 17
wide_sectors = 4
step_lefts = 2
whole_vmem = pl.BlockSpec(memory_space=pltpu.VMEM)
stays_out = pl.BlockSpec(memory_space=pltpu.HBM)


def gather_order(sectors):
    return gather_four if sectors == 4 else list(range(sectors))


def target_order(sectors):
    return target_four if sectors == 4 else list(range(sectors))


def first_order(sectors):
    return [i + at for at in (0, sectors) for i in (first_four if sectors == 4 else range(sectors))]


def place_in(order, distance):
    return sum(jnp.where(distance == far, place, 0) for place, far in enumerate(order))


def plan_length(slots):
    return -(-(slots + unroll_slots) // 128) * 128


def make_plan(sectors, lefts, rights, live, left_index, right_index, source, target, length):
    slots = left_index.shape[1]
    me = lax.axis_index("term")

    def columns_of(shape, dimension):
        return lax.broadcasted_iota(jnp.int32, shape, dimension)

    def total(chosen, values, axis):
        return jnp.sum(jnp.where(chosen, values, 0.0), axis=axis, keepdims=True)

    alive = columns_of((1, slots), 1) < live
    sent_at = place_in(target_order(sectors), target ^ me)
    group = jnp.where(alive, right_index * sectors + sent_at, rights * sectors).astype(jnp.float32)
    half = jnp.where(alive, place_in(gather_order(sectors), source ^ me) * lefts + left_index, 0).astype(jnp.float32)
    square = (slots, slots)
    one, two = columns_of(square, 0), columns_of(square, 1)
    group_here, half_here = (total(one == two, row, 1) for row in (group, half))
    earlier = (group == group_here) & (two < one)
    place = total((group < group_here) | earlier, 1.0, 1)
    goes_on = jnp.max(jnp.where(earlier, 1.0, 0.0), axis=1, keepdims=True)
    word = half_here + group_here * (1 << group_bit) + goes_on * (1 << last_bit)
    at = columns_of((slots, length), 1).astype(jnp.float32)
    sorted_words = total(place == at, word, 0).astype(jnp.int32)
    at = columns_of((1, length), 1)
    return jnp.where(at < slots, sorted_words, jnp.where(at == length - 1, live, (rights * sectors) << group_bit))


def half_products(sectors, left_ref, vector, halves):
    lefts, half_rows, columns = left_ref.shape
    left_all = left_ref.reshape(lefts * half_rows, columns)
    for first in range(0, sectors, wide_sectors):
        chosen = range(first, min(first + wide_sectors, sectors))
        wide = jnp.concatenate([vector[j] for j in chosen], axis=1)
        for left in range(0, lefts, step_lefts):
            rows = left_all[left * half_rows : (left + step_lefts) * half_rows, :]
            half = jnp.dot(rows, wide, preferred_element_type=jnp.float32).astype(jnp.bfloat16)
            for place, j in enumerate(chosen):
                part = half[:, place * columns : (place + 1) * columns]
                part = part.reshape(-1, half_rows, columns).astype(jnp.float32)
                halves[j * lefts + left : j * lefts + left + step_lefts] = part


def sum_halves(plan_ref, halves, sums):
    live = plan_ref[0, plan_ref.shape[1] - 1]

    def some_slots(turn, total):
        for step in range(unroll_slots):
            word = plan_ref[0, turn * unroll_slots + step]
            keep = (word >> last_bit).astype(jnp.float32)
            total = total * keep + halves[word & ((1 << group_bit) - 1)]
            sums[(word >> group_bit) & ((1 << (last_bit - group_bit)) - 1)] = total.astype(jnp.bfloat16)
        return total

    turns = (live + unroll_slots - 1) // unroll_slots
    lax.fori_loop(0, turns, some_slots, jnp.zeros(halves.shape[1:], jnp.float32))


def all_targets(sectors, right_ref, sums, out_refs):
    half_rows, columns = sums.shape[1:]
    product = 0
    for r in range(right_ref.shape[0]):
        rows = sums[r * sectors : (r + 1) * sectors].reshape(sectors * half_rows, columns)
        product = product + lax.dot_general(
            rows, right_ref[r], (((1,), (1,)), ((), ())), preferred_element_type=jnp.float32
        )
    for j in range(sectors):
        out_refs[j][...] = product[j * half_rows : (j + 1) * half_rows].astype(out_refs[j].dtype)


def join(core, vector, j, mine, other):
    rows = mine.shape[0]
    vector[j, pl.ds(pl.multiple_of(core * rows, rows), rows)] = mine
    vector[j, pl.ds(pl.multiple_of((1 - core) * rows, rows), rows)] = other


def wide_of(ref):
    return ref[...].astype(jnp.float32)


def prepare_kernel(sectors, count_ref, *refs):
    sources, kept, plan_ref = refs[:7], refs[7:10], refs[10]
    indices, arrived = refs[11:15], refs[15]
    copies = [pltpu.make_async_copy(*pair, arrived.at[i]) for i, pair in enumerate(zip(sources, (*indices, *kept)))]
    for copy in copies:
        copy.start()
    for copy in copies[:4]:
        copy.wait()
    lefts, rights = kept[0].shape[0], kept[1].shape[0]
    rows = [ref[...] for ref in indices]
    plan_ref[...] = make_plan(sectors, lefts, rights, count_ref[0], *rows, plan_ref.shape[1])
    for copy in copies[4:]:
        copy.wait()


def prepare(sectors, indices, count, arrays):
    sources = (*indices, *arrays)
    return pl.pallas_call(
        functools.partial(prepare_kernel, sectors),
        out_shape=[pltpu.VMEM(x.shape, x.dtype) for x in arrays]
        + [pltpu.VMEM((1, plan_length(indices[0].shape[1])), jnp.int32)],
        in_specs=[pl.BlockSpec(memory_space=pltpu.SMEM)] + [stays_out] * len(sources),
        out_specs=[whole_vmem] * (len(arrays) + 1),
        scratch_shapes=[pltpu.VMEM(x.shape, x.dtype) for x in indices] + [pltpu.SemaphoreType.DMA((len(sources),))],
    )(count, *(pltpu.with_memory_space_constraint(x, pltpu.HBM) for x in sources))


def first_kernel(sectors, plan_in, left, right, *refs):
    given, out_refs = refs[: 2 * sectors], refs[2 * sectors : -5]
    psis = [given[first_order(sectors).index(i)] for i in range(2 * sectors)]
    plan_ref, arrived, vector, halves, sums = refs[-5:]
    core = lax.axis_index("pair")
    plan_copy = pltpu.make_async_copy(plan_in, plan_ref, arrived)
    plan_copy.start()
    sums[...] = jnp.zeros_like(sums)
    for j in range(sectors):
        join(core, vector, j, psis[j][...], psis[sectors + j][...])
    half_products(sectors, left, vector, halves)
    plan_copy.wait()
    sum_halves(plan_ref, halves, sums)
    all_targets(sectors, right, sums, out_refs)


def second_kernel(sectors, plan_in, left, right, *refs):
    pieces = 2 * sectors
    psis, sigmas = refs[:pieces], refs[pieces : 2 * pieces]
    own_ref, *out_refs = refs[2 * pieces : -5]
    plan_ref, arrived, vector, halves, sums = refs[-5:]
    core = lax.axis_index("pair")
    plan_copy = pltpu.make_async_copy(plan_in, plan_ref, arrived)
    plan_copy.start()
    sums[...] = jnp.zeros_like(sums)
    norm = sum(wide_of(p) * wide_of(p) for p in psis)
    correlation = sum(wide_of(p) * wide_of(s) for p, s in zip(psis, sigmas))
    theta = jnp.sum(correlation) / jnp.sum(norm)
    square = jnp.zeros_like(norm)
    for p, s in zip(psis, sigmas):
        resid = wide_of(s) - theta * wide_of(p)
        square = square + resid * resid
    entries = pieces * norm.shape[0] * norm.shape[1]
    scale = lax.rsqrt(jnp.sum(square) / entries + 1e-06)
    for j in range(sectors):
        mine, other = (
            ((wide_of(sigmas[i]) - theta * wide_of(psis[i])) * scale).astype(jnp.bfloat16) for i in (j, sectors + j)
        )
        if j == 0:
            own_ref[...] = mine
        join(core, vector, j, mine, other)
    half_products(sectors, left, vector, halves)
    plan_copy.wait()
    sum_halves(plan_ref, halves, sums)
    all_targets(sectors, right, sums, out_refs)


def call_product(kernel, sectors, lefts, rights, inside, kept):
    half_rows, columns = inside[-1].shape
    shape = (half_rows, columns)
    block_bytes = half_rows * columns * 2
    outs = [*kept, pltpu.VMEM(shape, jnp.float32)] + [pltpu.VMEM(shape, jnp.bfloat16)] * (sectors - 1)
    return pl.pallas_call(
        functools.partial(kernel, sectors),
        out_shape=outs,
        in_specs=[whole_vmem] * len(inside),
        out_specs=[whole_vmem] * len(outs),
        scratch_shapes=[
            pltpu.SMEM(inside[0].shape, jnp.int32),
            pltpu.SemaphoreType.DMA,
            pltpu.VMEM((sectors, 2 * half_rows, columns), jnp.bfloat16),
            pltpu.VMEM((sectors * lefts, half_rows, columns), jnp.float32),
            pltpu.VMEM((sectors * rights + 1, half_rows, columns), jnp.bfloat16),
        ],
        compiler_params=pltpu.CompilerParams(
            vmem_limit_bytes=block_bytes * (sectors * (2 * lefts + rights + 24) + 64)
        ),
    )(*(pltpu.with_memory_space_constraint(x, pltpu.VMEM) for x in inside))


def swap(value, axis, bit):
    return lax.ppermute(value, axis, [(i, i ^ bit) for i in range(lax.axis_size(axis))])


def gather(own, kept):
    sectors = lax.axis_size("term")
    order = gather_order(sectors)
    mine = {0: kept}
    for j in reversed(range(1, sectors)):
        mine[j] = swap(own, "term", order[j])
    other = {j: swap(mine[j], "pair", 1) for j in (0, *reversed(range(1, sectors)))}
    return [mine[j] for j in range(sectors)] + [other[j] for j in range(sectors)]


def send(value, far, across):
    sectors, subs = lax.axis_size("term"), lax.axis_size("sub")
    route = [(t * subs + s, (t ^ far) * subs + (s ^ across)) for t in range(sectors) for s in range(subs)]
    return lax.ppermute(value, ("term", "sub"), route)


def owner_sum(parts):
    subs = lax.axis_size("sub")
    order = target_order(len(parts))
    direct = [far for far in order if far in direct_distances and subs == 2 and len(parts) == 4]
    total = parts[0]
    for place, far in enumerate(order):
        if place > 0 and far not in direct:
            total = total + send(parts[place], far, 0).astype(jnp.float32)
    beside = [send(parts[order.index(far)], far, across).astype(jnp.float32) for far in direct for across in range(subs)]
    bit = 1
    while bit < subs:
        rounded = total.astype(jnp.bfloat16)
        total = rounded.astype(jnp.float32) + send(rounded, 0, bit).astype(jnp.float32)
        bit *= 2
    for one, two in zip(beside[::2], beside[1::2]):
        total = total + (one + two)
    return total


def on_device(
    psi,
    left_blocks,
    right_blocks,
    left_index,
    right_index,
    block_source,
    block_target,
    block_count,
    sector_energy,
):
    sectors = lax.axis_size("term")
    lefts, rights = left_blocks.shape[1], right_blocks.shape[1]
    own = psi[0]
    indices = (left_index, right_index, block_source, block_target)
    left, right, own_kept, plan = prepare(sectors, indices, block_count, (left_blocks[0], right_blocks[0], own))
    psis = gather(own, own_kept)
    energy = sector_energy[0]
    call = functools.partial(call_product, sectors=sectors, lefts=lefts, rights=rights)
    handed = [psis[i] for i in first_order(sectors)]
    parts = call(first_kernel, inside=[plan, left, right, *handed], kept=[])
    sigma_first = (owner_sum(parts) + energy * own.astype(jnp.float32)).astype(jnp.bfloat16)
    correction, *parts = call(
        second_kernel,
        inside=[plan, left, right, *psis, *gather(sigma_first, sigma_first)],
        kept=[pltpu.VMEM(own.shape, own.dtype)],
    )
    sigma_second = (owner_sum(parts) + energy * correction.astype(jnp.float32)).astype(jnp.bfloat16)
    return (sigma_first[None], sigma_second[None])


def solution(mesh):
    placed = (
        P(("grp", "term"), "pair", None),
        P(("grp", "term", "sub"), None, "pair", None),
        P(("grp", "term", "sub"), None, None, None),
        P(("grp", "term", "sub"), None),
        P(("grp", "term", "sub"), None),
        P(("grp", "term", "sub"), None),
        P(("grp", "term", "sub"), None),
        P(("grp", "term", "sub")),
        P(("grp", "term")),
    )
    return jax.shard_map(
        on_device,
        mesh=mesh,
        in_specs=placed,
        out_specs=(P(("grp", "term"), "pair", None), P(("grp", "term"), "pair", None)),
        check_vma=False,
    )
```
